1024 devices in a mesh: row: 32 (over y, z_hi, core), col: 32 (over z_lo, x).
Axes of the slice: x: 4, y: 4, z: 32 (z_hi: 4, z_lo: 8; z = z_hi * 8 + z_lo), core: 2. Of those that a mesh axis runs over, the one named last changes fastest.
Arguments:
- left_tiles: bfloat16 [32, 32, 3, 128, 128], P('col', 'row'), may hold values from -0.5 to 0.5
- left_index: int32 [32, 32, 2, 3], P('col', 'row'), may hold values from -1 to 511, as said below
- right_tiles: bfloat16 [32, 32, 4, 128, 128], P('row', 'col'), may hold values from -6 to 6
- right_index: int32 [32, 32, 2, 4], P('row', 'col'), may hold values from -1 to 511, as said below
- keep_mask: int32 [32, 128], P('col', 'row'), may hold values 0 or 1
Outputs:
- product: bfloat16 [4096, 16384], P('col', 'row')
The draws below stay inside these ranges and needn't reach their ends.
Inputs may be any that keep to these rules, and one draw needn't show every extreme that they name: `left_index`: A slot is empty when both entries are -1, else its block-row lies in 0 to 0 and its block-column k satisfies k % 32 = (c + r) % 32 for the slot held at [c, r]. No two slots of one panel name the same block. Panels hold 1 or 3 tiles in their first slots; panel [0, 0] and some others are full. `right_index`: A slot is empty when both entries are -1, else its block-column lies in 0 to 3 and its block-row k satisfies k % 32 = (c + r) % 32 for the slot held at [r, c]. No two slots of one panel name the same block. Panels hold 1 or 4 tiles in their first slots; panel [0, 0] and some others are full.
All inputs are finite; a program needn't handle non-finite values. No bound on the sum of `keep_mask` on one device may be relied on, other than what follows from the above.
Results may differ from the reference program's by a relative error of at most 0.001.
Values may be sent and summed in bfloat16 or wider, within the bound.
No kernel may reach another device: no remote copies, remote signals or barrier semaphores. Data moves between devices by JAX's collectives and lax.ppermute only.
A program may use at most 32 MiB of HBM per device.

```python
import jax
import jax.numpy as jnp
from jax import lax

BS = 128
NB = 512
OCC_A = 3
OCC_B = 4
RB_DEV = 1
CB_DEV = 4
BAND = 32
COLS = 128
N_ROW = 32
N_COL = 32


def pick_cells(score_key, heavy_key, lead_a, lead_b, cells, slots):
    heavy_panel = jax.random.randint(heavy_key, (lead_a, lead_b), 0, 4) == 0
    heavy_panel = heavy_panel.at[0, 0].set(True)
    filled = jnp.where(heavy_panel, slots, 1)
    scores = jax.random.randint(score_key, (lead_a, lead_b, cells), 0, 1 << 16) * cells + jnp.arange(cells, dtype=jnp.int32)
    ranked = jnp.argsort(scores, axis=-1)[..., :slots].astype(jnp.int32)
    in_use = jnp.arange(slots, dtype=jnp.int32)[None, None, :] < filled[..., None]
    return (ranked, in_use)


def draw_left_index(key, part):
    key = jax.random.fold_in(key, 11)
    score_key, heavy_key = jax.random.split(key)
    key_slots = NB // N_ROW
    ranked, in_use = pick_cells(score_key, heavy_key, N_COL, N_ROW, RB_DEV * key_slots, OCC_A)
    band_row = ranked // key_slots
    aligned = (jnp.arange(N_COL, dtype=jnp.int32)[:, None] + jnp.arange(N_ROW, dtype=jnp.int32)[None, :]) % N_ROW
    block_key = ranked % key_slots * N_ROW + aligned[..., None]
    band_row = jnp.where(in_use, band_row, -1)
    block_key = jnp.where(in_use, block_key, -1)
    return jnp.stack([band_row, block_key], axis=2).astype(jnp.int32)


def draw_right_index(key, part):
    key = jax.random.fold_in(key, 23)
    score_key, heavy_key = jax.random.split(key)
    key_slots = NB // N_COL
    ranked, in_use = pick_cells(score_key, heavy_key, N_ROW, N_COL, key_slots * CB_DEV, OCC_B)
    aligned = (jnp.arange(N_ROW, dtype=jnp.int32)[:, None] + jnp.arange(N_COL, dtype=jnp.int32)[None, :]) % N_COL
    block_key = ranked // CB_DEV * N_COL + aligned[..., None]
    block_col = ranked % CB_DEV
    block_key = jnp.where(in_use, block_key, -1)
    block_col = jnp.where(in_use, block_col, -1)
    return jnp.stack([block_key, block_col], axis=2).astype(jnp.int32)


def plant(array, rng, smallest, largest):
    place = [jax.random.randint(jax.random.fold_in(rng, axis), (), 0, length) for axis, length in enumerate(array.shape)]
    widest = array.shape.index(max(array.shape))
    beside = place[:widest] + [(place[widest] + 1) % array.shape[widest]] + place[widest + 1:]
    return array.at[tuple(place)].set(smallest).at[tuple(beside)].set(largest)


def steps_of(key, dims, cuts, smallest, largest):
    loudness = 1.0
    for dim, blocks in cuts:
        steps = jax.random.uniform(jax.random.fold_in(jax.random.fold_in(key, 6), dim), (blocks,), jnp.float32, smallest / len(cuts), largest / len(cuts))
        loudness = loudness * jnp.repeat(jnp.exp(steps), dims[dim] // blocks).reshape((-1,) + (1,) * (len(dims) - 1 - dim))
    return loudness


def normal_values(own_key, extent, width, bound, shards=(), held_as=jnp.bfloat16):
    entries = jax.random.normal(own_key, extent, jnp.float32) * width
    if len(shards) > 0:
        entries = steps_of(own_key, extent, shards, -0.22, 0.18) * entries
    return jnp.clip(entries, min=-bound, max=bound).astype(held_as)


def setup_inputs(seed: int = 0) -> dict:
    streams_of = jax.random.split(jax.random.key(seed), 6)
    return {
        "left_tiles": normal_values(streams_of[0], (N_COL, N_ROW, OCC_A, BS, BS), BS ** -0.5, 0.5, ((0, 32), (1, 32))),
        "left_index": draw_left_index(jax.random.fold_in(streams_of[5], 71), 0),
        "right_tiles": normal_values(streams_of[2], (N_ROW, N_COL, OCC_B, BS, BS), 1.0, 6.0, ((0, 32), (1, 32))),
        "right_index": draw_right_index(jax.random.fold_in(streams_of[5], 71), 0),
        "keep_mask": plant((jax.random.randint(streams_of[4], (BAND, COLS), 0, 4) < 3).astype(jnp.int32), jax.random.fold_in(streams_of[4], 1), 0, 1),
    }


pair_block = 256


def reference(left_tiles, left_index, right_tiles, right_index, keep_mask):
    left_count = N_COL * N_ROW * OCC_A
    right_count = N_ROW * N_COL * OCC_B
    group_rows = (jnp.arange(N_COL, dtype=jnp.int32) * RB_DEV)[:, None, None]
    left_rows = jnp.where(left_index[:, :, 0, :] >= 0, group_rows + left_index[:, :, 0, :], -1).reshape(-1)
    left_keys = left_index[:, :, 1, :].reshape(-1)
    group_cols = (jnp.arange(N_ROW, dtype=jnp.int32) * CB_DEV)[:, None, None]
    right_keys = right_index[:, :, 0, :].reshape(-1)
    right_cols = jnp.where(right_index[:, :, 1, :] >= 0, group_cols + right_index[:, :, 1, :], -1).reshape(-1)
    left_flat = left_tiles.reshape(left_count, BS, BS)
    right_flat = right_tiles.reshape(right_count, BS, BS)
    matches = ((left_keys[:, None] == right_keys[None, :]) & (left_keys[:, None] >= 0)).reshape(-1).astype(jnp.int32)
    pair_order = jnp.argsort(1 - matches, stable=True).astype(jnp.int32)
    pair_order = jnp.concatenate([pair_order, jnp.zeros((pair_block,), jnp.int32)])
    live_pairs = jnp.sum(matches).astype(jnp.int32)

    def pending(carry_state):
        return carry_state[0] * pair_block < live_pairs

    def advance(carry_state):
        block_index, summed = carry_state
        first = (block_index * pair_block).astype(jnp.int32)
        picked = lax.dynamic_slice_in_dim(pair_order, first, pair_block)
        in_range = (first + jnp.arange(pair_block, dtype=jnp.int32)) < live_pairs
        left_pick = picked // right_count
        right_pick = picked % right_count
        products = jnp.einsum('pxy,pyz->pxz', left_flat[left_pick].astype(jnp.float32), right_flat[right_pick].astype(jnp.float32))
        target_rows = jnp.where(in_range, left_rows[left_pick], BAND)
        target_cols = jnp.where(in_range, right_cols[right_pick], COLS)
        summed = summed.at[target_rows, target_cols].add(products, mode='drop')
        return (block_index + 1, summed)

    summed = jnp.zeros((BAND, COLS, BS, BS), jnp.float32)
    finished = lax.while_loop(pending, advance, (jnp.zeros((), jnp.int32), summed))[1]
    finished = finished * keep_mask[:, :, None, None].astype(jnp.float32)
    return finished.transpose(0, 2, 1, 3).reshape(BAND * BS, COLS * BS).astype(jnp.bfloat16)
```

```python
import functools

import jax
import jax.numpy as jnp
from jax import lax
from jax.experimental import pallas as pl
from jax.experimental.pallas import tpu as pltpu
from jax.sharding import Mesh, PartitionSpec as P

ROW = ("y", "zh", "core")
COL = ("zl", "x")
GROUP = 32
TILE = 128
LEFT = 3
RIGHT = 4
PLACES = 16
PIECE = 2
MSG = RIGHT * PIECE
PANEL = LEFT * TILE
F32, BF16, I32 = jnp.float32, jnp.bfloat16, jnp.int32
VMEM_LIMIT = 48 * 1024 * 1024


def iota(shape, dim):
    return lax.broadcasted_iota(I32, shape, dim)


def scatter_kernel(place, left_ids, right_ids, keep, right, message, rows):
    row, col = place[0], place[1]
    for b in range(RIGHT):
        for u in range(4):
            strip = right[b, 32 * u : 32 * u + 32, :].astype(F32)
            rows[u % 2, pl.ds(PIECE * b + u // 2, GROUP, stride=MSG), :] = strip
    for v in range(2):
        message[:, :, v * TILE : (v + 1) * TILE] = rows[v].reshape(GROUP, MSG, TILE).astype(BF16)
    sub, lane = iota((MSG, TILE), 0), iota((MSG, TILE), 1)
    facts = jnp.zeros((MSG, TILE), I32)
    for b in range(RIGHT):
        key, block = right_ids[0, b], right_ids[1, b]
        here = lane == col * RIGHT + b
        facts = jnp.where((sub == 0) & here, jnp.where(key >= 0, lax.shift_right_logical(key, 5) + 1, 0), facts)
        facts = jnp.where((sub == 1) & here, block + 1, facts)
        facts = jnp.where((sub == 3) & (lane == b), keep[0, b], facts)
    for a in range(LEFT):
        key = left_ids[1, a]
        here = lane == row * LEFT + a
        facts = jnp.where((sub == 2) & here, jnp.where(key >= 0, lax.shift_right_logical(key, 5) + 1, 0), facts)
    facts = facts.astype(F32)
    message[:, :, 2 * TILE :] = jnp.broadcast_to(facts[None], (GROUP, MSG, TILE)).astype(BF16)


def left_kernel(left, pieces, payload, facts):
    facts[...] = pieces[:, :, 2 * TILE :].astype(F32).reshape(GROUP * MSG, TILE)
    ids = facts[pl.ds(2, GROUP, stride=MSG), :].astype(BF16)
    for n in range(payload.shape[0]):
        for a in range(LEFT):
            payload[n, a * TILE : (a + 1) * TILE, :] = left[a]
        payload[n, PANEL:, :] = ids


def select_kernel(place, pieces, left_facts, message, wanted, facts):
    row, col, base = place[0], place[1], place[2]
    facts[...] = pieces[:, :, 2 * TILE :].astype(F32).reshape(GROUP * MSG, TILE)
    right_q = jnp.sum(facts[pl.ds(0, GROUP, stride=MSG), :], axis=0, keepdims=True)
    right_j = jnp.sum(facts[pl.ds(1, GROUP, stride=MSG), :], axis=0, keepdims=True)
    keep = facts[pl.ds(3, GROUP, stride=MSG), :]
    left_q = jnp.sum(left_facts[...].astype(F32), axis=0)
    lane = iota((1, TILE), 1)
    right_class = ((lane >> 2) + row) & (GROUP - 1)
    right_key = jnp.where(right_q > 0, (right_q - 1) * GROUP + right_class.astype(F32), -2.0)
    slot = iota((GROUP, TILE), 1)
    left_class = (iota((GROUP, TILE), 0) + ((slot * 43) >> 7)) & (GROUP - 1)
    left_key = jnp.where(left_q > 0, (left_q - 1) * GROUP + left_class.astype(F32), -1.0)
    partner = jnp.full((GROUP, TILE), -1.0, F32)
    for t in range(GROUP * LEFT):
        partner = jnp.where(left_key[:, t : t + 1] == right_key, float(t), partner)
    kept = jnp.zeros((GROUP, TILE), F32)
    for j in range(RIGHT):
        kept = kept + jnp.where(right_j == j + 1, keep[:, j : j + 1], 0.0)
    needed = jnp.where((partner >= 0) & (kept > 0), 1.0, 0.0)
    before = (iota((TILE, TILE), 0) < iota((TILE, TILE), 1)).astype(F32).astype(BF16)
    order = jnp.dot(needed.astype(BF16), before, preferred_element_type=F32)
    spread = (iota((TILE, 2 * TILE), 0) == (iota((TILE, 2 * TILE), 1) >> 1)).astype(F32).astype(BF16)
    needed2 = jnp.dot(needed.astype(BF16), spread, preferred_element_type=F32)
    order2 = jnp.dot(order.astype(BF16), spread, preferred_element_type=F32)
    half = (iota((GROUP, 2 * TILE), 1) & 1).astype(F32)
    base_f = base.astype(F32)
    line = jnp.where(needed2 > 0, 2.0 * (order2 - base_f) + half, -1.0)
    lines = PIECE * PLACES
    chosen = line[:, None, :] == iota((GROUP, lines, 2 * TILE), 1).astype(F32)
    chosen = jnp.where(chosen, 1.0, 0.0).reshape(GROUP * lines, 2 * TILE).astype(BF16)
    held = pieces[:, :, 0 : 2 * TILE].astype(F32).reshape(GROUP * MSG, 2 * TILE).astype(BF16)
    packed = jnp.dot(chosen, held, preferred_element_type=F32)
    message[...] = packed.reshape(GROUP, lines, 2 * TILE).astype(BF16)
    most = jnp.max(jnp.where(needed > 0, order + 1.0, 0.0))
    own = iota((GROUP, TILE), 0) == col
    own_order = jnp.sum(jnp.where(own & (needed > 0), order + 1.0, 0.0), axis=0, keepdims=True)
    own_partner = jnp.sum(jnp.where(own, partner, 0.0), axis=0, keepdims=True)
    at = iota((PLACES, TILE), 0).astype(F32) + 1.0 + base_f
    here = own_order == at
    left_slot = jnp.sum(jnp.where(here, own_partner, 0.0), axis=1, keepdims=True)
    block = jnp.sum(jnp.where(here, right_j - 1.0, 0.0), axis=1, keepdims=True)
    live = jnp.sum(jnp.where(here, 1.0, 0.0), axis=1, keepdims=True)
    lane = iota((PLACES, TILE), 1)
    wanted[...] = jnp.where(
        lane == 0, left_slot, jnp.where(lane == 1, block, jnp.where(lane == 2, live, most))
    ).astype(I32)


def product_kernel(place, wanted, left_here, left_there, pieces, start, out, rows, total):
    lines = PIECE * PLACES
    for v in range(2):
        rows[v] = pieces[:, :, v * TILE : (v + 1) * TILE].astype(F32).reshape(GROUP * lines, TILE)
    if start is None:
        total[...] = jnp.zeros_like(total)
    else:
        total[...] = start[...]
    core = place[0] & 1
    for p in range(PLACES):

        @pl.when(wanted[p, 2] > 0)
        def _(p=p):
            tile = jnp.concatenate(
                [rows[u % 2, pl.ds(PIECE * p + u // 2, GROUP, stride=lines), :] for u in range(4)], axis=0
            ).astype(BF16)
            slot = wanted[p, 0]
            source = (slot * 43) >> 7
            a = pl.multiple_of((slot - source * LEFT) * TILE, TILE)
            panel = ((source >> 3) << 2) + ((source >> 1) & 3)
            columns = pl.ds(pl.multiple_of(wanted[p, 1] * TILE, TILE), TILE)

            @pl.when((source & 1) == core)
            def _():
                total[:, columns] += jnp.dot(left_here[panel, pl.ds(a, TILE), :], tile, preferred_element_type=F32)

            @pl.when((source & 1) != core)
            def _():
                total[:, columns] += jnp.dot(left_there[panel, pl.ds(a, TILE), :], tile, preferred_element_type=F32)

    out[...] = total[...].astype(out.dtype)


def kernel_call(body, out_shape, scratch, in_smem, *operands):
    specs = [pl.BlockSpec(memory_space=pltpu.SMEM if i < in_smem else pltpu.VMEM) for i in range(len(operands))]
    many = isinstance(out_shape, tuple)
    vmem = pl.BlockSpec(memory_space=pltpu.VMEM)
    return pl.pallas_call(
        body,
        out_shape=out_shape,
        in_specs=specs,
        out_specs=tuple(vmem for _ in out_shape) if many else vmem,
        scratch_shapes=scratch,
        compiler_params=pltpu.CompilerParams(vmem_limit_bytes=VMEM_LIMIT),
    )(*operands)


def on_device(left_tiles, left_index, right_tiles, right_index, keep_mask):
    row, col = lax.axis_index(ROW), lax.axis_index(COL)
    place = jnp.stack([row, col, 0]).astype(I32)
    lines = PIECE * PLACES

    with jax.named_scope("scatter_right"):
        message = kernel_call(
            scatter_kernel,
            jax.ShapeDtypeStruct((GROUP, MSG, 3 * TILE), BF16),
            [pltpu.VMEM((2, GROUP * MSG, TILE), F32)],
            4,
            place,
            left_index[0, 0],
            right_index[0, 0],
            keep_mask,
            right_tiles[0, 0],
        )
        pieces = lax.all_to_all(message, COL, 0, 0, tiled=True)

    with jax.named_scope("left_zh"):
        zh = lax.axis_size("zh")
        payload = kernel_call(
            left_kernel,
            jax.ShapeDtypeStruct((zh, PANEL + GROUP, TILE), BF16),
            [pltpu.VMEM((GROUP * MSG, TILE), F32)],
            0,
            left_tiles[0, 0],
            pieces,
        )
        slab = lax.all_to_all(payload, "zh", 0, 0, tiled=True)

    with jax.named_scope("left_ids"):
        ids = jnp.sum(slab[:, PANEL:, :].astype(F32), axis=0).astype(BF16)
        near = ("y", "core")
        ids = jnp.broadcast_to(ids[None], (lax.axis_size(near), GROUP, TILE))
        ids = lax.all_to_all(ids, near, 0, 0, tiled=True)

    with jax.named_scope("left_y"):
        left_here = lax.all_gather(slab, "y").reshape(-1, PANEL + GROUP, TILE)
    with jax.named_scope("left_core"):
        left_there = lax.ppermute(left_here, "core", [(0, 1), (1, 0)])

    def select(base):
        return kernel_call(
            select_kernel,
            (
                jax.ShapeDtypeStruct((GROUP, lines, 2 * TILE), BF16),
                jax.ShapeDtypeStruct((PLACES, TILE), I32),
            ),
            [pltpu.VMEM((GROUP * MSG, TILE), F32)],
            1,
            jnp.stack([row, col, base]).astype(I32),
            pieces,
            ids,
        )

    def product(wanted, tiles, start, dtype):
        shape = (TILE, RIGHT * TILE)
        operands = (place, wanted, left_here, left_there, tiles) + (() if start is None else (start,))
        body = product_kernel
        if start is None:
            body = lambda a, b, c, d, e, out, *scratch: product_kernel(a, b, c, d, e, None, out, *scratch)
        return kernel_call(
            body,
            jax.ShapeDtypeStruct(shape, dtype),
            [pltpu.VMEM((2, GROUP * lines, TILE), F32), pltpu.VMEM(shape, F32)],
            2,
            *operands,
        )

    with jax.named_scope("right_needed"):
        packed, wanted = select(jnp.int32(0))
        tiles = lax.all_to_all(packed, COL, 0, 0, tiled=True)
    with jax.named_scope("multiply"):
        first = product(wanted, tiles, None, BF16)

    most = wanted[0, 3]

    def more_rounds(_):
        def one(carry):
            base, total = carry
            packed, wanted = select(base)
            tiles = lax.all_to_all(packed, COL, 0, 0, tiled=True)
            return base + PLACES, product(wanted, tiles, total, F32)

        begin = (jnp.int32(0), jnp.zeros((TILE, RIGHT * TILE), F32))
        return lax.while_loop(lambda carry: carry[0] < most, one, begin)[1].astype(BF16)

    with jax.named_scope("further_rounds"):
        return lax.cond(most > PLACES, more_rounds, lambda done: done, first)


def solution(mesh):
    parts = Mesh(mesh.devices.reshape(4, 4, 2, 8, 4), ROW + COL)
    in_specs = (P(COL, ROW), P(COL, ROW), P(ROW, COL), P(ROW, COL), P(COL, ROW))
    return jax.shard_map(on_device, mesh=parts, in_specs=in_specs, out_specs=P(COL, ROW), check_vma=False)
```

```python
import functools

import jax
import jax.numpy as jnp
from jax import lax
from jax.experimental import pallas as pl
from jax.experimental.pallas import tpu as pltpu
from jax.sharding import Mesh, PartitionSpec as P

ROW = ("y", "zh", "core")
HALF = ("zl", "x")
COL = ("zb",) + HALF
GROUP = 32
TILE = 128
LEFT = 3
RIGHT = 4
PLACES = 16
SPREAD = 16
WIDE = 4
PIECE = TILE // SPREAD // WIDE
MSG = RIGHT * PIECE
PANEL = LEFT * TILE
IDS = 16
F32, BF16, I32 = jnp.float32, jnp.bfloat16, jnp.int32
VMEM_LIMIT = 48 * 1024 * 1024


def iota(shape, dim):
    return lax.broadcasted_iota(I32, shape, dim)


def scatter_kernel(place, right_ids, keep, right, data, own_facts, rows):
    for b in range(RIGHT):
        for u in range(TILE // SPREAD):
            strip = right[b, SPREAD * u : SPREAD * (u + 1), :].astype(F32)
            rows[u % WIDE, pl.ds(PIECE * b + u // WIDE, SPREAD, stride=MSG), :] = strip
    for v in range(WIDE):
        data[:, :, v * TILE : (v + 1) * TILE] = rows[v].reshape(SPREAD, MSG, TILE).astype(BF16)
    sub, lane = iota((MSG, TILE), 0), iota((MSG, TILE), 1)
    facts = jnp.zeros((MSG, TILE), I32)
    for b in range(RIGHT):
        key, block = right_ids[0, b], right_ids[1, b]
        here = lane == place[1] * RIGHT + b
        facts = jnp.where((sub == 0) & here, jnp.where(key >= 0, lax.shift_right_logical(key, 5) + 1, 0), facts)
        facts = jnp.where((sub == 1) & here, block + 1, facts)
        facts = jnp.where((sub == 3) & (lane == b), keep[0, b], facts)
    own_facts[...] = facts.astype(F32)


def message_kernel(data, own_facts, left_ids, message):
    for half in range(GROUP // SPREAD):
        message[half * SPREAD : (half + 1) * SPREAD, :, 0 : WIDE * TILE] = data[...]
    left_q = jnp.sum(left_ids[:, 0:MSG, :].astype(F32), axis=0)[0:1]
    facts = jnp.where(iota((MSG, TILE), 0) == 2, left_q, own_facts[...])
    message[:, :, WIDE * TILE :] = jnp.broadcast_to(facts[None], (GROUP, MSG, TILE)).astype(BF16)


def left_kernel(place, ids, left, payload):
    for a in range(LEFT):
        payload[a * TILE : (a + 1) * TILE, :] = left[a]
    lane = iota((IDS, TILE), 1)
    facts = jnp.zeros((IDS, TILE), I32)
    for a in range(LEFT):
        key = ids[1, a]
        here = (iota((IDS, TILE), 0) == 0) & (lane == place[0] * LEFT + a)
        facts = jnp.where(here, jnp.where(key >= 0, lax.shift_right_logical(key, 5) + 1, 0), facts)
    payload[PANEL:, :] = facts.astype(F32).astype(BF16)


def select_kernel(place, pieces, below, above, message, wanted, facts):
    row, col, base = place[0], place[1], place[2]
    first = (col // SPREAD) * SPREAD
    facts[...] = pieces[:, :, WIDE * TILE :].astype(F32).reshape(GROUP * MSG, TILE)
    right_q = jnp.sum(facts[pl.ds(0, GROUP, stride=MSG), :], axis=0, keepdims=True)
    right_j = jnp.sum(facts[pl.ds(1, GROUP, stride=MSG), :], axis=0, keepdims=True)
    keep = facts[pl.ds(first * MSG + 3, SPREAD, stride=MSG), :]
    left_q = facts[pl.ds(first * MSG + 2, SPREAD, stride=MSG), :]
    lane = iota((1, TILE), 1)
    right_class = ((lane >> 2) + row) & (GROUP - 1)
    right_key = jnp.where(right_q > 0, (right_q - 1) * GROUP + right_class.astype(F32), -2.0)
    slot = iota((SPREAD, TILE), 1)
    left_class = (first + iota((SPREAD, TILE), 0) + ((slot * 43) >> 7)) & (GROUP - 1)
    left_key = jnp.where(left_q > 0, (left_q - 1) * GROUP + left_class.astype(F32), -1.0)
    partner = jnp.full((SPREAD, TILE), -1.0, F32)
    for t in range(GROUP * LEFT):
        partner = jnp.where(left_key[:, t : t + 1] == right_key, float(t), partner)
    kept = jnp.zeros((SPREAD, TILE), F32)
    for j in range(RIGHT):
        kept = kept + jnp.where(right_j == j + 1, keep[:, j : j + 1], 0.0)
    needed = jnp.where((partner >= 0) & (kept > 0), 1.0, 0.0)
    before = (iota((TILE, TILE), 0) < iota((TILE, TILE), 1)).astype(F32).astype(BF16)
    order = jnp.dot(needed.astype(BF16), before, preferred_element_type=F32)
    spread = (iota((TILE, 2 * TILE), 0) == (iota((TILE, 2 * TILE), 1) >> 1)).astype(F32).astype(BF16)
    needed2 = jnp.dot(needed.astype(BF16), spread, preferred_element_type=F32)
    order2 = jnp.dot(order.astype(BF16), spread, preferred_element_type=F32)
    half = (iota((SPREAD, 2 * TILE), 1) & 1).astype(F32)
    base_f = base.astype(F32)
    line = jnp.where(needed2 > 0, 2.0 * (order2 - base_f) + half, -1.0)
    lines = PIECE * PLACES
    chosen = line[:, None, :] == iota((SPREAD, lines, 2 * TILE), 1).astype(F32)
    chosen = jnp.where(chosen, 1.0, 0.0).reshape(SPREAD * lines, 2 * TILE).astype(BF16)
    held = pieces[:, :, 0 : WIDE * TILE].astype(F32).reshape(GROUP * MSG, WIDE * TILE).astype(BF16)
    packed = jnp.dot(chosen, held, preferred_element_type=F32)
    message[...] = packed.reshape(SPREAD, lines, WIDE * TILE).astype(BF16)
    most = jnp.max(jnp.where(needed > 0, order + 1.0, 0.0))
    own = iota((SPREAD, TILE), 0) == col - first
    own_order = jnp.sum(jnp.where(own & (needed > 0), order + 1.0, 0.0), axis=0, keepdims=True)
    own_partner = jnp.sum(jnp.where(own, partner, 0.0), axis=0, keepdims=True)
    at = iota((PLACES, TILE), 0).astype(F32) + 1.0 + base_f
    here = own_order == at
    left_slot = jnp.sum(jnp.where(here, own_partner, 0.0), axis=1, keepdims=True)
    block = jnp.sum(jnp.where(here, right_j - 1.0, 0.0), axis=1, keepdims=True)
    live = jnp.sum(jnp.where(here, 1.0, 0.0), axis=1, keepdims=True)
    lane = iota((PLACES, TILE), 1)
    wanted[...] = jnp.where(
        lane == 0, left_slot, jnp.where(lane == 1, block, jnp.where(lane == 2, live, most))
    ).astype(I32)


def product_kernel(place, wanted, left_here, left_there, pieces, start, out, rows, total):
    lines = PIECE * PLACES
    for v in range(WIDE):
        rows[v] = pieces[:, :, v * TILE : (v + 1) * TILE].astype(F32).reshape(SPREAD * lines, TILE)
    if start is None:
        total[...] = jnp.zeros_like(total)
    else:
        total[...] = start[...]
    core = place[0] & 1
    for p in range(PLACES):

        @pl.when(wanted[p, 2] > 0)
        def _(p=p):
            tile = jnp.concatenate(
                [rows[u % WIDE, pl.ds(PIECE * p + u // WIDE, SPREAD, stride=lines), :] for u in range(TILE // SPREAD)],
                axis=0,
            ).astype(BF16)
            slot = wanted[p, 0]
            source = (slot * 43) >> 7
            a = pl.multiple_of((slot - source * LEFT) * TILE, TILE)
            panel = ((((place[0] >> 3) - (source >> 3)) & 3) << 2) + ((source >> 1) & 3)
            columns = pl.ds(pl.multiple_of(wanted[p, 1] * TILE, TILE), TILE)

            @pl.when((source & 1) == core)
            def _():
                total[:, columns] += jnp.dot(left_here[panel, pl.ds(a, TILE), :], tile, preferred_element_type=F32)

            @pl.when((source & 1) != core)
            def _():
                total[:, columns] += jnp.dot(left_there[panel, pl.ds(a, TILE), :], tile, preferred_element_type=F32)

    out[...] = total[...].astype(out.dtype)


def kernel_call(body, out_shape, scratch, spaces, *operands):
    kinds = {"s": pltpu.SMEM, "v": pltpu.VMEM, "a": pl.ANY}
    specs = [pl.BlockSpec(memory_space=kinds[space]) for space in spaces]
    many = isinstance(out_shape, tuple)
    vmem = pl.BlockSpec(memory_space=pltpu.VMEM)
    return pl.pallas_call(
        body,
        out_shape=out_shape,
        in_specs=specs,
        out_specs=tuple(vmem for _ in out_shape) if many else vmem,
        scratch_shapes=scratch,
        compiler_params=pltpu.CompilerParams(vmem_limit_bytes=VMEM_LIMIT),
    )(*operands)


def on_device(left_tiles, left_index, right_tiles, right_index, keep_mask):
    row, col = lax.axis_index(ROW), lax.axis_index(COL)
    place = jnp.stack([row, col, 0]).astype(I32)
    lines = PIECE * PLACES

    with jax.named_scope("left_zh"):
        payload = kernel_call(
            left_kernel,
            jax.ShapeDtypeStruct((PANEL + IDS, TILE), BF16),
            [],
            "ssv",
            place,
            left_index[0, 0],
            left_tiles[0, 0],
        )
        slab = lax.all_gather(payload, "zh")

    with jax.named_scope("left_ids"):
        ids = jnp.sum(slab[:, PANEL:, :].astype(F32), axis=0).astype(BF16)
        near = ("y", "core")
        ids = jnp.broadcast_to(ids[None], (lax.axis_size(near), IDS, TILE))
        ids = lax.all_to_all(ids, near, 0, 0, tiled=True)

    with jax.named_scope("scatter_right"):
        data, own_facts = kernel_call(
            scatter_kernel,
            (
                jax.ShapeDtypeStruct((SPREAD, MSG, WIDE * TILE), BF16),
                jax.ShapeDtypeStruct((MSG, TILE), F32),
            ),
            [pltpu.VMEM((WIDE, SPREAD * MSG, TILE), F32)],
            "sssv",
            place,
            right_index[0, 0],
            keep_mask,
            right_tiles[0, 0],
        )
        message = kernel_call(
            message_kernel,
            jax.ShapeDtypeStruct((GROUP, MSG, (WIDE + 1) * TILE), BF16),
            [],
            "vvv",
            data,
            own_facts,
            ids,
        )
        pieces = lax.all_to_all(message, COL, 0, 0, tiled=True)

    with jax.named_scope("left_y"):
        size = lax.axis_size("y")
        up = [(i, (i + 1) % size) for i in range(size)]
        down = [(i, (i - 1) % size) for i in range(size)]
        half = slab.shape[0] // 2
        below = lax.ppermute(slab, "y", up)
        above = lax.ppermute(slab, "y", down)
        far = (lax.ppermute(below[:half], "y", up), lax.ppermute(above[half:], "y", down))
        left_here = jnp.concatenate((slab, below) + far + (above,))

    with jax.named_scope("left_core"):
        left_there = lax.ppermute(left_here, "core", [(0, 1), (1, 0)])

    def select(base):
        return kernel_call(
            select_kernel,
            (
                jax.ShapeDtypeStruct((SPREAD, lines, WIDE * TILE), BF16),
                jax.ShapeDtypeStruct((PLACES, TILE), I32),
            ),
            [pltpu.VMEM((GROUP * MSG, TILE), F32)],
            "svaa",
            jnp.stack([row, col, base]).astype(I32),
            pieces,
            below,
            above,
        )

    def product(wanted, tiles, start, dtype):
        shape = (TILE, RIGHT * TILE)
        operands = (place, wanted, left_here, left_there, tiles) + (() if start is None else (start,))
        body = product_kernel
        if start is None:
            body = lambda a, b, c, d, e, out, *scratch: product_kernel(a, b, c, d, e, None, out, *scratch)
        return kernel_call(
            body,
            jax.ShapeDtypeStruct(shape, dtype),
            [pltpu.VMEM((WIDE, SPREAD * lines, TILE), F32), pltpu.VMEM(shape, F32)],
            "ssvvvv"[: len(operands)],
            *operands,
        )

    with jax.named_scope("right_needed"):
        packed, wanted = select(jnp.int32(0))
        tiles = lax.all_to_all(packed, HALF, 0, 0, tiled=True)
    with jax.named_scope("multiply"):
        first = product(wanted, tiles, None, BF16)

    most = wanted[0, 3]

    def more_rounds(_):
        def one(carry):
            base, total = carry
            packed, wanted = select(base)
            tiles = lax.all_to_all(packed, HALF, 0, 0, tiled=True)
            return base + PLACES, product(wanted, tiles, total, F32)

        begin = (jnp.int32(0), jnp.zeros((TILE, RIGHT * TILE), F32))
        return lax.while_loop(lambda carry: carry[0] < most, one, begin)[1].astype(BF16)

    with jax.named_scope("further_rounds"):
        return lax.cond(most > PLACES, more_rounds, lambda done: done, first)


def solution(mesh):
    parts = Mesh(mesh.devices.reshape(4, 4, 2, 2, 4, 4), ROW + COL)
    in_specs = (P(COL, ROW), P(COL, ROW), P(ROW, COL), P(ROW, COL), P(COL, ROW))
    return jax.shard_map(on_device, mesh=parts, in_specs=in_specs, out_specs=P(COL, ROW), check_vma=False)
```

```python
import functools

import jax
import jax.numpy as jnp
from jax import lax
from jax.experimental import pallas as pl
from jax.experimental.pallas import tpu as pltpu
from jax.sharding import Mesh, PartitionSpec as P

ROW = ("y", "zh", "core")
HALF = ("zl", "x")
COL = ("zb",) + HALF
GROUP = 32
TILE = 128
LEFT = 3
RIGHT = 4
PLACES = 16
SPREAD = 16
WIDE = 4
PIECE = TILE // SPREAD // WIDE
MSG = RIGHT * PIECE
PANEL = LEFT * TILE
IDS = 16
F32, BF16, I32 = jnp.float32, jnp.bfloat16, jnp.int32
VMEM_LIMIT = 48 * 1024 * 1024


def iota(shape, dim):
    return lax.broadcasted_iota(I32, shape, dim)


def scatter_kernel(place, right_ids, keep, right, data, own_facts, rows):
    for b in range(RIGHT):
        for u in range(TILE // SPREAD):
            strip = right[b, SPREAD * u : SPREAD * (u + 1), :].astype(F32)
            rows[u % WIDE, pl.ds(PIECE * b + u // WIDE, SPREAD, stride=MSG), :] = strip
    for v in range(WIDE):
        data[:, :, v * TILE : (v + 1) * TILE] = rows[v].reshape(SPREAD, MSG, TILE).astype(BF16)
    sub, lane = iota((MSG, TILE), 0), iota((MSG, TILE), 1)
    facts = jnp.zeros((MSG, TILE), I32)
    for b in range(RIGHT):
        key, block = right_ids[0, b], right_ids[1, b]
        here = lane == place[1] * RIGHT + b
        facts = jnp.where((sub == 0) & here, jnp.where(key >= 0, lax.shift_right_logical(key, 5) + 1, 0), facts)
        facts = jnp.where((sub == 1) & here, block + 1, facts)
        facts = jnp.where((sub == 3) & (lane == b), keep[0, b], facts)
    own_facts[...] = facts.astype(F32)


def message_kernel(data, own_facts, left_ids, message):
    for half in range(GROUP // SPREAD):
        message[half * SPREAD : (half + 1) * SPREAD, :, 0 : WIDE * TILE] = data[...]
    left_q = jnp.sum(left_ids[:, 0:MSG, :].astype(F32), axis=0)[0:1]
    facts = jnp.where(iota((MSG, TILE), 0) == 2, left_q, own_facts[...])
    message[:, :, WIDE * TILE :] = jnp.broadcast_to(facts[None], (GROUP, MSG, TILE)).astype(BF16)


def left_kernel(near_ids, left, facts, payload):
    for a in range(LEFT):
        payload[a * TILE : (a + 1) * TILE, :] = left[a]
    payload[PANEL:, :] = jnp.sum(near_ids[...].astype(F32), axis=0).astype(BF16)


def select_kernel(place, pieces, below, above, message, wanted, facts):
    row, col, base = place[0], place[1], place[2]
    first = (col // SPREAD) * SPREAD
    facts[...] = pieces[:, :, WIDE * TILE :].astype(F32).reshape(GROUP * MSG, TILE)
    right_q = jnp.sum(facts[pl.ds(0, GROUP, stride=MSG), :], axis=0, keepdims=True)
    right_j = jnp.sum(facts[pl.ds(1, GROUP, stride=MSG), :], axis=0, keepdims=True)
    keep = facts[pl.ds(first * MSG + 3, SPREAD, stride=MSG), :]
    left_q = facts[pl.ds(first * MSG + 2, SPREAD, stride=MSG), :]
    lane = iota((1, TILE), 1)
    right_class = ((lane >> 2) + row) & (GROUP - 1)
    right_key = jnp.where(right_q > 0, (right_q - 1) * GROUP + right_class.astype(F32), -2.0)
    slot = iota((SPREAD, TILE), 1)
    left_class = (first + iota((SPREAD, TILE), 0) + ((slot * 43) >> 7)) & (GROUP - 1)
    left_key = jnp.where(left_q > 0, (left_q - 1) * GROUP + left_class.astype(F32), -1.0)
    partner = jnp.full((SPREAD, TILE), -1.0, F32)
    for t in range(GROUP * LEFT):
        partner = jnp.where(left_key[:, t : t + 1] == right_key, float(t), partner)
    kept = jnp.zeros((SPREAD, TILE), F32)
    for j in range(RIGHT):
        kept = kept + jnp.where(right_j == j + 1, keep[:, j : j + 1], 0.0)
    needed = jnp.where((partner >= 0) & (kept > 0), 1.0, 0.0)
    before = (iota((TILE, TILE), 0) < iota((TILE, TILE), 1)).astype(F32).astype(BF16)
    order = jnp.dot(needed.astype(BF16), before, preferred_element_type=F32)
    spread = (iota((TILE, 2 * TILE), 0) == (iota((TILE, 2 * TILE), 1) >> 1)).astype(F32).astype(BF16)
    needed2 = jnp.dot(needed.astype(BF16), spread, preferred_element_type=F32)
    order2 = jnp.dot(order.astype(BF16), spread, preferred_element_type=F32)
    half = (iota((SPREAD, 2 * TILE), 1) & 1).astype(F32)
    base_f = base.astype(F32)
    line = jnp.where(needed2 > 0, 2.0 * (order2 - base_f) + half, -1.0)
    lines = PIECE * PLACES
    chosen = line[:, None, :] == iota((SPREAD, lines, 2 * TILE), 1).astype(F32)
    chosen = jnp.where(chosen, 1.0, 0.0).reshape(SPREAD * lines, 2 * TILE).astype(BF16)
    held = pieces[:, :, 0 : WIDE * TILE].astype(F32).reshape(GROUP * MSG, WIDE * TILE).astype(BF16)
    packed = jnp.dot(chosen, held, preferred_element_type=F32)
    message[...] = packed.reshape(SPREAD, lines, WIDE * TILE).astype(BF16)
    most = jnp.max(jnp.where(needed > 0, order + 1.0, 0.0))
    own = iota((SPREAD, TILE), 0) == col - first
    own_order = jnp.sum(jnp.where(own & (needed > 0), order + 1.0, 0.0), axis=0, keepdims=True)
    own_partner = jnp.sum(jnp.where(own, partner, 0.0), axis=0, keepdims=True)
    at = iota((PLACES, TILE), 0).astype(F32) + 1.0 + base_f
    here = own_order == at
    left_slot = jnp.sum(jnp.where(here, own_partner, 0.0), axis=1, keepdims=True)
    block = jnp.sum(jnp.where(here, right_j - 1.0, 0.0), axis=1, keepdims=True)
    live = jnp.sum(jnp.where(here, 1.0, 0.0), axis=1, keepdims=True)
    lane = iota((PLACES, TILE), 1)
    wanted[...] = jnp.where(
        lane == 0, left_slot, jnp.where(lane == 1, block, jnp.where(lane == 2, live, most))
    ).astype(I32)


def product_kernel(place, wanted, left_here, left_there, pieces, start, out, rows, total):
    lines = PIECE * PLACES
    for v in range(WIDE):
        rows[v] = pieces[:, :, v * TILE : (v + 1) * TILE].astype(F32).reshape(SPREAD * lines, TILE)
    if start is None:
        total[...] = jnp.zeros_like(total)
    else:
        total[...] = start[...]
    core = place[0] & 1
    for p in range(PLACES):

        @pl.when(wanted[p, 2] > 0)
        def _(p=p):
            tile = jnp.concatenate(
                [rows[u % WIDE, pl.ds(PIECE * p + u // WIDE, SPREAD, stride=lines), :] for u in range(TILE // SPREAD)],
                axis=0,
            ).astype(BF16)
            slot = wanted[p, 0]
            source = (slot * 43) >> 7
            a = pl.multiple_of((slot - source * LEFT) * TILE, TILE)
            panel = ((((place[0] >> 3) - (source >> 3)) & 3) << 2) + ((source >> 1) & 3)
            columns = pl.ds(pl.multiple_of(wanted[p, 1] * TILE, TILE), TILE)

            @pl.when((source & 1) == core)
            def _():
                total[:, columns] += jnp.dot(left_here[panel, pl.ds(a, TILE), :], tile, preferred_element_type=F32)

            @pl.when((source & 1) != core)
            def _():
                total[:, columns] += jnp.dot(left_there[panel, pl.ds(a, TILE), :], tile, preferred_element_type=F32)

    out[...] = total[...].astype(out.dtype)


def kernel_call(body, out_shape, scratch, spaces, *operands):
    kinds = {"s": pltpu.SMEM, "v": pltpu.VMEM, "a": pl.ANY}
    specs = [pl.BlockSpec(memory_space=kinds[space]) for space in spaces]
    many = isinstance(out_shape, tuple)
    vmem = pl.BlockSpec(memory_space=pltpu.VMEM)
    return pl.pallas_call(
        body,
        out_shape=out_shape,
        in_specs=specs,
        out_specs=tuple(vmem for _ in out_shape) if many else vmem,
        scratch_shapes=scratch,
        compiler_params=pltpu.CompilerParams(vmem_limit_bytes=VMEM_LIMIT),
    )(*operands)


def on_device(left_tiles, left_index, right_tiles, right_index, keep_mask):
    row, col = lax.axis_index(ROW), lax.axis_index(COL)
    place = jnp.stack([row, col, 0]).astype(I32)
    lines = PIECE * PLACES

    with jax.named_scope("left_ids"):
        key = left_index[0, 0, 1]
        values = jnp.where(key >= 0, lax.shift_right_logical(key, 5) + 1, 0)
        here = iota((LEFT, TILE), 1) == row * LEFT + iota((LEFT, TILE), 0)
        ids = jnp.sum(jnp.where(here, values[:, None], 0), axis=0).astype(F32).astype(BF16)
        near = ("y", "core")
        near_ids = jnp.broadcast_to(ids[None, None], (lax.axis_size(near), IDS, TILE))
        near_ids = lax.all_to_all(near_ids, near, 0, 0, tiled=True)

    with jax.named_scope("scatter_right"):
        data, own_facts = kernel_call(
            scatter_kernel,
            (
                jax.ShapeDtypeStruct((SPREAD, MSG, WIDE * TILE), BF16),
                jax.ShapeDtypeStruct((MSG, TILE), F32),
            ),
            [pltpu.VMEM((WIDE, SPREAD * MSG, TILE), F32)],
            "sssv",
            place,
            right_index[0, 0],
            keep_mask,
            right_tiles[0, 0],
        )
    with jax.named_scope("left_zh"):
        payload = kernel_call(
            left_kernel,
            jax.ShapeDtypeStruct((PANEL + IDS, TILE), BF16),
            [],
            "vva",
            near_ids,
            left_tiles[0, 0],
            own_facts,
        )
        slab = lax.all_gather(payload, "zh")

    with jax.named_scope("right_message"):
        message = kernel_call(
            message_kernel,
            jax.ShapeDtypeStruct((GROUP, MSG, (WIDE + 1) * TILE), BF16),
            [],
            "vvv",
            data,
            own_facts,
            slab[:, PANEL:, :],
        )
        pieces = lax.all_to_all(message, COL, 0, 0, tiled=True)

    with jax.named_scope("left_y"):
        size = lax.axis_size("y")
        up = [(i, (i + 1) % size) for i in range(size)]
        down = [(i, (i - 1) % size) for i in range(size)]
        half = slab.shape[0] // 2
        below = lax.ppermute(slab, "y", up)
        above = lax.ppermute(slab, "y", down)
        far = (lax.ppermute(below[:half], "y", up), lax.ppermute(above[half:], "y", down))
        left_here = jnp.concatenate((slab, below) + far + (above,))

    with jax.named_scope("left_core"):
        left_there = lax.ppermute(left_here, "core", [(0, 1), (1, 0)])

    def select(base):
        return kernel_call(
            select_kernel,
            (
                jax.ShapeDtypeStruct((SPREAD, lines, WIDE * TILE), BF16),
                jax.ShapeDtypeStruct((PLACES, TILE), I32),
            ),
            [pltpu.VMEM((GROUP * MSG, TILE), F32)],
            "svaa",
            jnp.stack([row, col, base]).astype(I32),
            pieces,
            below,
            above,
        )

    def product(wanted, tiles, start, dtype):
        shape = (TILE, RIGHT * TILE)
        operands = (place, wanted, left_here, left_there, tiles) + (() if start is None else (start,))
        body = product_kernel
        if start is None:
            body = lambda a, b, c, d, e, out, *scratch: product_kernel(a, b, c, d, e, None, out, *scratch)
        return kernel_call(
            body,
            jax.ShapeDtypeStruct(shape, dtype),
            [pltpu.VMEM((WIDE, SPREAD * lines, TILE), F32), pltpu.VMEM(shape, F32)],
            "ssvvvv"[: len(operands)],
            *operands,
        )

    with jax.named_scope("right_needed"):
        packed, wanted = select(jnp.int32(0))
        tiles = lax.all_to_all(packed, HALF, 0, 0, tiled=True)
    with jax.named_scope("multiply"):
        first = product(wanted, tiles, None, BF16)

    most = wanted[0, 3]

    def more_rounds(_):
        def one(carry):
            base, total = carry
            packed, wanted = select(base)
            tiles = lax.all_to_all(packed, HALF, 0, 0, tiled=True)
            return base + PLACES, product(wanted, tiles, total, F32)

        begin = (jnp.int32(0), jnp.zeros((TILE, RIGHT * TILE), F32))
        return lax.while_loop(lambda carry: carry[0] < most, one, begin)[1].astype(BF16)

    with jax.named_scope("further_rounds"):
        return lax.cond(most > PLACES, more_rounds, lambda done: done, first)


def solution(mesh):
    parts = Mesh(mesh.devices.reshape(4, 4, 2, 2, 4, 4), ROW + COL)
    in_specs = (P(COL, ROW), P(COL, ROW), P(ROW, COL), P(ROW, COL), P(COL, ROW))
    return jax.shard_map(on_device, mesh=parts, in_specs=in_specs, out_specs=P(COL, ROW), check_vma=False)
```

```python
import functools

import jax
import jax.numpy as jnp
from jax import lax
from jax.experimental import pallas as pl
from jax.experimental.pallas import tpu as pltpu
from jax.sharding import Mesh, PartitionSpec as P

ROW = ("y", "zh", "core")
HALF = ("zl", "x")
COL = ("zb",) + HALF
GROUP = 32
TILE = 128
LEFT = 3
RIGHT = 4
PLACES = 16
SPREAD = 16
WIDE = 4
PIECE = TILE // SPREAD // WIDE
MSG = RIGHT * PIECE
PANEL = LEFT * TILE
IDS = 16
F32, BF16, I32 = jnp.float32, jnp.bfloat16, jnp.int32
VMEM_LIMIT = 48 * 1024 * 1024


def iota(shape, dim):
    return lax.broadcasted_iota(I32, shape, dim)


def scatter_kernel(place, right_ids, keep, right, data, own_facts, rows):
    for b in range(RIGHT):
        for u in range(TILE // SPREAD):
            strip = right[b, SPREAD * u : SPREAD * (u + 1), :].astype(F32)
            rows[u % WIDE, pl.ds(PIECE * b + u // WIDE, SPREAD, stride=MSG), :] = strip
    for v in range(WIDE):
        data[:, :, v * TILE : (v + 1) * TILE] = rows[v].reshape(SPREAD, MSG, TILE).astype(BF16)
    sub, lane = iota((MSG, TILE), 0), iota((MSG, TILE), 1)
    facts = jnp.zeros((MSG, TILE), I32)
    for b in range(RIGHT):
        key, block = right_ids[0, b], right_ids[1, b]
        here = lane == place[1] * RIGHT + b
        facts = jnp.where((sub == 0) & here, jnp.where(key >= 0, lax.shift_right_logical(key, 5) + 1, 0), facts)
        facts = jnp.where((sub == 1) & here, block + 1, facts)
        facts = jnp.where((sub == 3) & (lane == b), keep[0, b], facts)
    own_facts[...] = facts.astype(F32)


def message_kernel(data, own_facts, left_ids, message):
    for half in range(GROUP // SPREAD):
        message[half * SPREAD : (half + 1) * SPREAD, :, 0 : WIDE * TILE] = data[...]
    left_q = jnp.sum(left_ids[:, 0:MSG, :].astype(F32), axis=0)[0:1]
    facts = jnp.where(iota((MSG, TILE), 0) == 2, left_q, own_facts[...])
    message[:, :, WIDE * TILE :] = jnp.broadcast_to(facts[None], (GROUP, MSG, TILE)).astype(BF16)


def left_kernel(near_ids, left, facts, payload):
    for a in range(LEFT):
        payload[a * TILE : (a + 1) * TILE, :] = left[a]
    payload[PANEL:, :] = jnp.sum(near_ids[...].astype(F32), axis=0).astype(BF16)


def select_kernel(place, pieces, below, above, message, wanted, facts):
    row, col, base = place[0], place[1], place[2]
    first = (col // SPREAD) * SPREAD
    facts[...] = pieces[:, :, WIDE * TILE :].astype(F32).reshape(GROUP * MSG, TILE)
    right_q = jnp.sum(facts[pl.ds(0, GROUP, stride=MSG), :], axis=0, keepdims=True)
    right_j = jnp.sum(facts[pl.ds(1, GROUP, stride=MSG), :], axis=0, keepdims=True)
    keep = facts[pl.ds(first * MSG + 3, SPREAD, stride=MSG), :]
    left_q = facts[pl.ds(first * MSG + 2, SPREAD, stride=MSG), :]
    lane = iota((1, TILE), 1)
    right_class = ((lane >> 2) + row) & (GROUP - 1)
    right_key = jnp.where(right_q > 0, (right_q - 1) * GROUP + right_class.astype(F32), -2.0)
    slot = iota((SPREAD, TILE), 1)
    left_class = (first + iota((SPREAD, TILE), 0) + ((slot * 43) >> 7)) & (GROUP - 1)
    left_key = jnp.where(left_q > 0, (left_q - 1) * GROUP + left_class.astype(F32), -1.0)
    partner = jnp.full((SPREAD, TILE), -1.0, F32)
    for t in range(GROUP * LEFT):
        partner = jnp.where(left_key[:, t : t + 1] == right_key, float(t), partner)
    kept = jnp.zeros((SPREAD, TILE), F32)
    for j in range(RIGHT):
        kept = kept + jnp.where(right_j == j + 1, keep[:, j : j + 1], 0.0)
    needed = jnp.where((partner >= 0) & (kept > 0), 1.0, 0.0)
    before = (iota((TILE, TILE), 0) < iota((TILE, TILE), 1)).astype(F32).astype(BF16)
    order = jnp.dot(needed.astype(BF16), before, preferred_element_type=F32)
    spread = (iota((TILE, 2 * TILE), 0) == (iota((TILE, 2 * TILE), 1) >> 1)).astype(F32).astype(BF16)
    needed2 = jnp.dot(needed.astype(BF16), spread, preferred_element_type=F32)
    order2 = jnp.dot(order.astype(BF16), spread, preferred_element_type=F32)
    half = (iota((SPREAD, 2 * TILE), 1) & 1).astype(F32)
    base_f = base.astype(F32)
    line = jnp.where(needed2 > 0, 2.0 * (order2 - base_f) + half, -1.0)
    lines = PIECE * PLACES
    chosen = line[:, None, :] == iota((SPREAD, lines, 2 * TILE), 1).astype(F32)
    chosen = jnp.where(chosen, 1.0, 0.0).reshape(SPREAD * lines, 2 * TILE).astype(BF16)
    held = pieces[:, :, 0 : WIDE * TILE].astype(F32).reshape(GROUP * MSG, WIDE * TILE).astype(BF16)
    packed = jnp.dot(chosen, held, preferred_element_type=F32)
    message[...] = packed.reshape(SPREAD, lines, WIDE * TILE).astype(BF16)
    most = jnp.max(jnp.where(needed > 0, order + 1.0, 0.0))
    own = iota((SPREAD, TILE), 0) == col - first
    own_order = jnp.sum(jnp.where(own & (needed > 0), order + 1.0, 0.0), axis=0, keepdims=True)
    own_partner = jnp.sum(jnp.where(own, partner, 0.0), axis=0, keepdims=True)
    at = iota((PLACES, TILE), 0).astype(F32) + 1.0 + base_f
    here = own_order == at
    left_slot = jnp.sum(jnp.where(here, own_partner, 0.0), axis=1, keepdims=True)
    block = jnp.sum(jnp.where(here, right_j - 1.0, 0.0), axis=1, keepdims=True)
    live = jnp.sum(jnp.where(here, 1.0, 0.0), axis=1, keepdims=True)
    lane = iota((PLACES, TILE), 1)
    wanted[...] = jnp.where(
        lane == 0, left_slot, jnp.where(lane == 1, block, jnp.where(lane == 2, live, most))
    ).astype(I32)


def product_kernel(place, wanted, left_here, left_there, pieces, start, out, rows, total):
    lines = PIECE * PLACES
    for v in range(WIDE):
        rows[v] = pieces[:, :, v * TILE : (v + 1) * TILE].astype(F32).reshape(SPREAD * lines, TILE)
    if start is None:
        total[...] = jnp.zeros_like(total)
    else:
        total[...] = start[...]
    core = place[0] & 1
    for p in range(PLACES):

        @pl.when(wanted[p, 2] > 0)
        def _(p=p):
            tile = jnp.concatenate(
                [rows[u % WIDE, pl.ds(PIECE * p + u // WIDE, SPREAD, stride=lines), :] for u in range(TILE // SPREAD)],
                axis=0,
            ).astype(BF16)
            slot = wanted[p, 0]
            source = (slot * 43) >> 7
            a = pl.multiple_of((slot - source * LEFT) * TILE, TILE)
            panel = ((((place[0] >> 3) - (source >> 3)) & 3) << 2) + ((source >> 1) & 3)
            columns = pl.ds(pl.multiple_of(wanted[p, 1] * TILE, TILE), TILE)

            @pl.when((source & 1) == core)
            def _():
                total[:, columns] += jnp.dot(left_here[panel, pl.ds(a, TILE), :], tile, preferred_element_type=F32)

            @pl.when((source & 1) != core)
            def _():
                total[:, columns] += jnp.dot(left_there[panel, pl.ds(a, TILE), :], tile, preferred_element_type=F32)

    out[...] = total[...].astype(out.dtype)


def kernel_call(body, out_shape, scratch, spaces, *operands):
    kinds = {"s": pltpu.SMEM, "v": pltpu.VMEM, "a": pl.ANY}
    specs = [pl.BlockSpec(memory_space=kinds[space]) for space in spaces]
    many = isinstance(out_shape, tuple)
    vmem = pl.BlockSpec(memory_space=pltpu.VMEM)
    return pl.pallas_call(
        body,
        out_shape=out_shape,
        in_specs=specs,
        out_specs=tuple(vmem for _ in out_shape) if many else vmem,
        scratch_shapes=scratch,
        compiler_params=pltpu.CompilerParams(vmem_limit_bytes=VMEM_LIMIT),
    )(*operands)


def on_device(left_tiles, left_index, right_tiles, right_index, keep_mask):
    row, col = lax.axis_index(ROW), lax.axis_index(COL)
    place = jnp.stack([row, col, 0]).astype(I32)
    lines = PIECE * PLACES

    with jax.named_scope("left_ids"):
        key = left_index[0, 0, 1]
        values = jnp.where(key >= 0, lax.shift_right_logical(key, 5) + 1, 0)
        here = iota((LEFT, TILE), 1) == row * LEFT + iota((LEFT, TILE), 0)
        ids = jnp.sum(jnp.where(here, values[:, None], 0), axis=0).astype(F32).astype(BF16)
        near = ("y", "core")
        near_ids = jnp.broadcast_to(ids[None, None], (lax.axis_size(near), IDS, TILE))
        near_ids = lax.all_to_all(near_ids, near, 0, 0, tiled=True)

    with jax.named_scope("scatter_right"):
        data, own_facts = kernel_call(
            scatter_kernel,
            (
                jax.ShapeDtypeStruct((SPREAD, MSG, WIDE * TILE), BF16),
                jax.ShapeDtypeStruct((MSG, TILE), F32),
            ),
            [pltpu.VMEM((WIDE, SPREAD * MSG, TILE), F32)],
            "sssv",
            place,
            right_index[0, 0],
            keep_mask,
            right_tiles[0, 0],
        )
    with jax.named_scope("left_zh"):
        payload = kernel_call(
            left_kernel,
            jax.ShapeDtypeStruct((PANEL + IDS, TILE), BF16),
            [],
            "vva",
            near_ids,
            left_tiles[0, 0],
            own_facts,
        )
        slab = lax.all_gather(payload, "zh")

    with jax.named_scope("right_message"):
        message = kernel_call(
            message_kernel,
            jax.ShapeDtypeStruct((GROUP, MSG, (WIDE + 1) * TILE), BF16),
            [],
            "vvv",
            data,
            own_facts,
            slab[:, PANEL:, :],
        )
        pieces = lax.all_to_all(message, COL, 0, 0, tiled=True)

    with jax.named_scope("left_y"):
        size = lax.axis_size("y")
        up = [(i, (i + 1) % size) for i in range(size)]
        down = [(i, (i - 1) % size) for i in range(size)]
        ring = [(2 * y + core, (y + 1 - 2 * core) % size * 2 + core) for y in range(size) for core in range(2)]
        below = lax.ppermute(slab, "y", up)
        above = lax.ppermute(slab, "y", down)
        onward = jnp.where(lax.axis_index("core") == 0, below, above)
        far = lax.ppermute(onward, ("y", "core"), ring)
        left_here = jnp.concatenate((slab, below, far, above))

    with jax.named_scope("left_core"):
        left_there = lax.ppermute(left_here, "core", [(0, 1), (1, 0)])

    def select(base):
        return kernel_call(
            select_kernel,
            (
                jax.ShapeDtypeStruct((SPREAD, lines, WIDE * TILE), BF16),
                jax.ShapeDtypeStruct((PLACES, TILE), I32),
            ),
            [pltpu.VMEM((GROUP * MSG, TILE), F32)],
            "svaa",
            jnp.stack([row, col, base]).astype(I32),
            pieces,
            below,
            above,
        )

    def product(wanted, tiles, start, dtype):
        shape = (TILE, RIGHT * TILE)
        operands = (place, wanted, left_here, left_there, tiles) + (() if start is None else (start,))
        body = product_kernel
        if start is None:
            body = lambda a, b, c, d, e, out, *scratch: product_kernel(a, b, c, d, e, None, out, *scratch)
        return kernel_call(
            body,
            jax.ShapeDtypeStruct(shape, dtype),
            [pltpu.VMEM((WIDE, SPREAD * lines, TILE), F32), pltpu.VMEM(shape, F32)],
            "ssvvvv"[: len(operands)],
            *operands,
        )

    with jax.named_scope("right_needed"):
        packed, wanted = select(jnp.int32(0))
        tiles = lax.all_to_all(packed, HALF, 0, 0, tiled=True)
    with jax.named_scope("multiply"):
        first = product(wanted, tiles, None, BF16)

    most = wanted[0, 3]

    def more_rounds(_):
        def one(carry):
            base, total = carry
            packed, wanted = select(base)
            tiles = lax.all_to_all(packed, HALF, 0, 0, tiled=True)
            return base + PLACES, product(wanted, tiles, total, F32)

        begin = (jnp.int32(0), jnp.zeros((TILE, RIGHT * TILE), F32))
        return lax.while_loop(lambda carry: carry[0] < most, one, begin)[1].astype(BF16)

    with jax.named_scope("further_rounds"):
        return lax.cond(most > PLACES, more_rounds, lambda done: done, first)


def solution(mesh):
    parts = Mesh(mesh.devices.reshape(4, 4, 2, 2, 4, 4), ROW + COL)
    in_specs = (P(COL, ROW), P(COL, ROW), P(ROW, COL), P(ROW, COL), P(COL, ROW))
    return jax.shard_map(on_device, mesh=parts, in_specs=in_specs, out_specs=P(COL, ROW), check_vma=False)
```

```python
import functools

import jax
import jax.numpy as jnp
from jax import lax
from jax.experimental import pallas as pl
from jax.experimental.pallas import tpu as pltpu
from jax.sharding import Mesh, PartitionSpec as P

ROW = ("y", "zh", "core")
HALF = ("zl", "x")
COL = ("zb",) + HALF
GROUP = 32
TILE = 128
LEFT = 3
RIGHT = 4
PLACES = 16
SPREAD = 16
WIDE = 4
PIECE = TILE // SPREAD // WIDE
MSG = RIGHT * PIECE
PANEL = LEFT * TILE
IDS = 16
F32, BF16, I32 = jnp.float32, jnp.bfloat16, jnp.int32
VMEM_LIMIT = 48 * 1024 * 1024


def iota(shape, dim):
    return lax.broadcasted_iota(I32, shape, dim)


def scatter_kernel(place, right_ids, keep, right, data, own_facts, rows):
    for b in range(RIGHT):
        for u in range(TILE // SPREAD):
            strip = right[b, SPREAD * u : SPREAD * (u + 1), :].astype(F32)
            rows[u % WIDE, pl.ds(PIECE * b + u // WIDE, SPREAD, stride=MSG), :] = strip
    for v in range(WIDE):
        data[:, :, v * TILE : (v + 1) * TILE] = rows[v, 0 : SPREAD * MSG, :].reshape(SPREAD, MSG, TILE).astype(BF16)
    sub, lane = iota((MSG, TILE), 0), iota((MSG, TILE), 1)
    facts = jnp.zeros((MSG, TILE), I32)
    for b in range(RIGHT):
        key, block = right_ids[0, b], right_ids[1, b]
        here = lane == place[1] * RIGHT + b
        facts = jnp.where((sub == 0) & here, jnp.where(key >= 0, lax.shift_right_logical(key, 5) + 1, 0), facts)
        facts = jnp.where((sub == 1) & here, block + 1, facts)
        facts = jnp.where((sub == 3) & (lane == b), keep[0, b], facts)
    own_facts[...] = facts.astype(F32)


def message_kernel(data, own_facts, left_ids, message):
    for half in range(GROUP // SPREAD):
        message[half * SPREAD : (half + 1) * SPREAD, :, 0 : WIDE * TILE] = data[...]
    left_q = jnp.sum(left_ids[:, 0:MSG, :].astype(F32), axis=0)[0:1]
    facts = jnp.where(iota((MSG, TILE), 0) == 2, left_q, own_facts[...])
    message[:, :, WIDE * TILE :] = jnp.broadcast_to(facts[None], (GROUP, MSG, TILE)).astype(BF16)


def left_kernel(near_ids, left, facts, payload):
    for a in range(LEFT):
        payload[a * TILE : (a + 1) * TILE, :] = left[a]
    payload[PANEL:, :] = jnp.sum(near_ids[...].astype(F32), axis=0).astype(BF16)


def select_kernel(place, pieces, below, above, message, wanted, facts):
    row, col, base = place[0], place[1], place[2]
    first = (col // SPREAD) * SPREAD
    facts[0 : GROUP * MSG, :] = pieces[:, :, WIDE * TILE :].astype(F32).reshape(GROUP * MSG, TILE)
    right_q = jnp.sum(facts[pl.ds(0, GROUP, stride=MSG), :], axis=0, keepdims=True)
    right_j = jnp.sum(facts[pl.ds(1, GROUP, stride=MSG), :], axis=0, keepdims=True)
    keep = facts[pl.ds(first * MSG + 3, SPREAD, stride=MSG), :]
    left_q = facts[pl.ds(first * MSG + 2, SPREAD, stride=MSG), :]
    lane = iota((1, TILE), 1)
    right_class = ((lane >> 2) + row) & (GROUP - 1)
    right_key = jnp.where(right_q > 0, (right_q - 1) * GROUP + right_class.astype(F32), -2.0)
    slot = iota((SPREAD, TILE), 1)
    left_class = (first + iota((SPREAD, TILE), 0) + ((slot * 43) >> 7)) & (GROUP - 1)
    left_key = jnp.where(left_q > 0, (left_q - 1) * GROUP + left_class.astype(F32), -1.0)
    partner = jnp.full((SPREAD, TILE), -1.0, F32)
    for t in range(GROUP * LEFT):
        partner = jnp.where(left_key[:, t : t + 1] == right_key, float(t), partner)
    kept = jnp.zeros((SPREAD, TILE), F32)
    for j in range(RIGHT):
        kept = kept + jnp.where(right_j == j + 1, keep[:, j : j + 1], 0.0)
    needed = jnp.where((partner >= 0) & (kept > 0), 1.0, 0.0)
    before = (iota((TILE, TILE), 0) < iota((TILE, TILE), 1)).astype(F32).astype(BF16)
    order = jnp.dot(needed.astype(BF16), before, preferred_element_type=F32)
    spread = (iota((TILE, 2 * TILE), 0) == (iota((TILE, 2 * TILE), 1) >> 1)).astype(F32).astype(BF16)
    needed2 = jnp.dot(needed.astype(BF16), spread, preferred_element_type=F32)
    order2 = jnp.dot(order.astype(BF16), spread, preferred_element_type=F32)
    half = (iota((SPREAD, 2 * TILE), 1) & 1).astype(F32)
    base_f = base.astype(F32)
    line = jnp.where(needed2 > 0, 2.0 * (order2 - base_f) + half, -1.0)
    lines = PIECE * PLACES
    chosen = line[:, None, :] == iota((SPREAD, lines, 2 * TILE), 1).astype(F32)
    chosen = jnp.where(chosen, 1.0, 0.0).reshape(SPREAD * lines, 2 * TILE).astype(BF16)
    held = pieces[:, :, 0 : WIDE * TILE].astype(F32).reshape(GROUP * MSG, WIDE * TILE).astype(BF16)
    packed = jnp.dot(chosen, held, preferred_element_type=F32)
    message[...] = packed.reshape(SPREAD, lines, WIDE * TILE).astype(BF16)
    most = jnp.max(jnp.where(needed > 0, order + 1.0, 0.0))
    own = iota((SPREAD, TILE), 0) == col - first
    own_order = jnp.sum(jnp.where(own & (needed > 0), order + 1.0, 0.0), axis=0, keepdims=True)
    own_partner = jnp.sum(jnp.where(own, partner, 0.0), axis=0, keepdims=True)
    at = iota((PLACES, TILE), 0).astype(F32) + 1.0 + base_f
    here = own_order == at
    left_slot = jnp.sum(jnp.where(here, own_partner, 0.0), axis=1, keepdims=True)
    block = jnp.sum(jnp.where(here, right_j - 1.0, 0.0), axis=1, keepdims=True)
    live = jnp.sum(jnp.where(here, 1.0, 0.0), axis=1, keepdims=True)
    lane = iota((PLACES, TILE), 1)
    wanted[...] = jnp.where(
        lane == 0, left_slot, jnp.where(lane == 1, block, jnp.where(lane == 2, live, most))
    ).astype(I32)


def product_kernel(place, wanted, left_here, left_there, pieces, start, out, rows, total):
    lines = PIECE * PLACES
    for v in range(WIDE):
        rows[v, 0 : SPREAD * lines, :] = pieces[:, :, v * TILE : (v + 1) * TILE].astype(F32).reshape(SPREAD * lines, TILE)
    if start is None:
        total[...] = jnp.zeros_like(total)
    else:
        total[...] = start[...]
    core = place[0] & 1
    for p in range(PLACES):

        @pl.when(wanted[p, 2] > 0)
        def _(p=p):
            tile = jnp.concatenate(
                [rows[u % WIDE, pl.ds(PIECE * p + u // WIDE, SPREAD, stride=lines), :] for u in range(TILE // SPREAD)],
                axis=0,
            ).astype(BF16)
            slot = wanted[p, 0]
            source = (slot * 43) >> 7
            a = pl.multiple_of((slot - source * LEFT) * TILE, TILE)
            panel = ((((place[0] >> 3) - (source >> 3)) & 3) << 2) + ((source >> 1) & 3)
            columns = pl.ds(pl.multiple_of(wanted[p, 1] * TILE, TILE), TILE)

            @pl.when((source & 1) == core)
            def _():
                total[:, columns] += jnp.dot(left_here[panel, pl.ds(a, TILE), :], tile, preferred_element_type=F32)

            @pl.when((source & 1) != core)
            def _():
                total[:, columns] += jnp.dot(left_there[panel, pl.ds(a, TILE), :], tile, preferred_element_type=F32)

    out[...] = total[...].astype(out.dtype)


def kernel_call(body, out_shape, scratch, spaces, *operands):
    kinds = {"s": pltpu.SMEM, "v": pltpu.VMEM, "a": pl.ANY}
    specs = [pl.BlockSpec(memory_space=kinds[space]) for space in spaces]
    many = isinstance(out_shape, tuple)
    vmem = pl.BlockSpec(memory_space=pltpu.VMEM)
    return pl.pallas_call(
        body,
        out_shape=out_shape,
        in_specs=specs,
        out_specs=tuple(vmem for _ in out_shape) if many else vmem,
        scratch_shapes=scratch,
        compiler_params=pltpu.CompilerParams(vmem_limit_bytes=VMEM_LIMIT),
    )(*operands)


def on_device(left_tiles, left_index, right_tiles, right_index, keep_mask):
    row, col = lax.axis_index(ROW), lax.axis_index(COL)
    place = jnp.stack([row, col, 0]).astype(I32)
    lines = PIECE * PLACES

    with jax.named_scope("left_ids"):
        key = left_index[0, 0, 1]
        values = jnp.where(key >= 0, lax.shift_right_logical(key, 5) + 1, 0)
        here = iota((LEFT, TILE), 1) == row * LEFT + iota((LEFT, TILE), 0)
        ids = jnp.sum(jnp.where(here, values[:, None], 0), axis=0).astype(F32).astype(BF16)
        near = ("y", "core")
        near_ids = jnp.broadcast_to(ids[None, None], (lax.axis_size(near), IDS, TILE))
        near_ids = lax.all_to_all(near_ids, near, 0, 0, tiled=True)

    with jax.named_scope("scatter_right"):
        data, own_facts = kernel_call(
            scatter_kernel,
            (
                jax.ShapeDtypeStruct((SPREAD, MSG, WIDE * TILE), BF16),
                jax.ShapeDtypeStruct((MSG, TILE), F32),
            ),
            [pltpu.VMEM((WIDE, (SPREAD + 1) * MSG, TILE), F32)],
            "sssv",
            place,
            right_index[0, 0],
            keep_mask,
            right_tiles[0, 0],
        )
    with jax.named_scope("left_zh"):
        payload = kernel_call(
            left_kernel,
            jax.ShapeDtypeStruct((PANEL + IDS, TILE), BF16),
            [],
            "vva",
            near_ids,
            left_tiles[0, 0],
            own_facts,
        )
        slab = lax.all_gather(payload, "zh")

    with jax.named_scope("right_message"):
        message = kernel_call(
            message_kernel,
            jax.ShapeDtypeStruct((GROUP, MSG, (WIDE + 1) * TILE), BF16),
            [],
            "vvv",
            data,
            own_facts,
            slab[:, PANEL:, :],
        )
        pieces = lax.all_to_all(message, COL, 0, 0, tiled=True)

    with jax.named_scope("left_y"):
        size = lax.axis_size("y")
        up = [(i, (i + 1) % size) for i in range(size)]
        down = [(i, (i - 1) % size) for i in range(size)]
        ring = [(2 * y + core, (y + 1 - 2 * core) % size * 2 + core) for y in range(size) for core in range(2)]
        below = lax.ppermute(slab, "y", up)
        above = lax.ppermute(slab, "y", down)
        onward = jnp.where(lax.axis_index("core") == 0, below, above)
        far = lax.ppermute(onward, ("y", "core"), ring)
        left_here = jnp.concatenate((slab, below, far, above))

    with jax.named_scope("left_core"):
        left_there = lax.ppermute(left_here, "core", [(0, 1), (1, 0)])

    def select(base):
        return kernel_call(
            select_kernel,
            (
                jax.ShapeDtypeStruct((SPREAD, lines, WIDE * TILE), BF16),
                jax.ShapeDtypeStruct((PLACES, TILE), I32),
            ),
            [pltpu.VMEM(((GROUP + 1) * MSG, TILE), F32)],
            "svaa",
            jnp.stack([row, col, base]).astype(I32),
            pieces,
            below,
            above,
        )

    def product(wanted, tiles, start, dtype):
        shape = (TILE, RIGHT * TILE)
        operands = (place, wanted, left_here, left_there, tiles) + (() if start is None else (start,))
        body = product_kernel
        if start is None:
            body = lambda a, b, c, d, e, out, *scratch: product_kernel(a, b, c, d, e, None, out, *scratch)
        return kernel_call(
            body,
            jax.ShapeDtypeStruct(shape, dtype),
            [pltpu.VMEM((WIDE, (SPREAD + 1) * lines, TILE), F32), pltpu.VMEM(shape, F32)],
            "ssvvvv"[: len(operands)],
            *operands,
        )

    with jax.named_scope("right_needed"):
        packed, wanted = select(jnp.int32(0))
        tiles = lax.all_to_all(packed, HALF, 0, 0, tiled=True)
    with jax.named_scope("multiply"):
        first = product(wanted, tiles, None, BF16)

    most = wanted[0, 3]

    def more_rounds(_):
        def one(carry):
            base, total = carry
            packed, wanted = select(base)
            tiles = lax.all_to_all(packed, HALF, 0, 0, tiled=True)
            return base + PLACES, product(wanted, tiles, total, F32)

        begin = (jnp.int32(0), jnp.zeros((TILE, RIGHT * TILE), F32))
        return lax.while_loop(lambda carry: carry[0] < most, one, begin)[1].astype(BF16)

    with jax.named_scope("further_rounds"):
        return lax.cond(most > PLACES, more_rounds, lambda done: done, first)


def solution(mesh):
    parts = Mesh(mesh.devices.reshape(4, 4, 2, 2, 4, 4), ROW + COL)
    in_specs = (P(COL, ROW), P(COL, ROW), P(ROW, COL), P(ROW, COL), P(COL, ROW))
    return jax.shard_map(on_device, mesh=parts, in_specs=in_specs, out_specs=P(COL, ROW), check_vma=False)
```

```python
import functools

import jax
import jax.numpy as jnp
from jax import lax
from jax.experimental import pallas as pl
from jax.experimental.pallas import tpu as pltpu
from jax.sharding import Mesh, PartitionSpec as P

ROW = ("y", "zh", "core")
HALF = ("zl", "x")
COL = ("zb",) + HALF
GROUP = 32
TILE = 128
LEFT = 3
RIGHT = 4
PLACES = 16
SPREAD = 16
WIDE = 4
PIECE = TILE // SPREAD // WIDE
MSG = RIGHT * PIECE
PANEL = LEFT * TILE
IDS = 8
F32, BF16, I32 = jnp.float32, jnp.bfloat16, jnp.int32
VMEM_LIMIT = 48 * 1024 * 1024


def iota(shape, dim):
    return lax.broadcasted_iota(I32, shape, dim)


def scatter_kernel(place, right_ids, keep, right, data, own_facts, rows):
    for b in range(RIGHT):
        for u in range(TILE // SPREAD):
            strip = right[b, SPREAD * u : SPREAD * (u + 1), :].astype(F32)
            rows[u % WIDE, pl.ds(PIECE * b + u // WIDE, SPREAD, stride=MSG), :] = strip
    for v in range(WIDE):
        data[:, :, v * TILE : (v + 1) * TILE] = rows[v, 0 : SPREAD * MSG, :].reshape(SPREAD, MSG, TILE).astype(BF16)
    sub, lane = iota((MSG, TILE), 0), iota((MSG, TILE), 1)
    facts = jnp.zeros((MSG, TILE), I32)
    for b in range(RIGHT):
        key, block = right_ids[0, b], right_ids[1, b]
        here = lane == place[1] * RIGHT + b
        facts = jnp.where((sub == 0) & here, jnp.where(key >= 0, lax.shift_right_logical(key, 5) + 1, 0), facts)
        facts = jnp.where((sub == 1) & here, block + 1, facts)
        facts = jnp.where((sub == 3) & (lane == b), keep[0, b], facts)
    own_facts[...] = facts.astype(F32)


def message_kernel(data, own_facts, left_ids, message):
    for half in range(GROUP // SPREAD):
        message[half * SPREAD : (half + 1) * SPREAD, :, 0 : WIDE * TILE] = data[...]
    left_q = jnp.sum(left_ids[:, 0:MSG, :].astype(F32), axis=0)[0:1]
    facts = jnp.where(iota((MSG, TILE), 0) == 2, left_q, own_facts[...])
    message[:, :, WIDE * TILE :] = jnp.broadcast_to(facts[None], (GROUP, MSG, TILE)).astype(BF16)


def left_kernel(near_ids, left, facts, payload):
    for a in range(LEFT):
        payload[a * TILE : (a + 1) * TILE, :] = left[a]
    payload[PANEL:, :] = jnp.sum(near_ids[...].astype(F32), axis=0).astype(BF16)


def select_kernel(place, pieces, below, above, message, wanted, facts):
    row, col, base = place[0], place[1], place[2]
    first = (col // SPREAD) * SPREAD
    facts[0 : GROUP * MSG, :] = pieces[:, :, WIDE * TILE :].astype(F32).reshape(GROUP * MSG, TILE)
    right_q = jnp.sum(facts[pl.ds(0, GROUP, stride=MSG), :], axis=0, keepdims=True)
    right_j = jnp.sum(facts[pl.ds(1, GROUP, stride=MSG), :], axis=0, keepdims=True)
    keep = facts[pl.ds(first * MSG + 3, SPREAD, stride=MSG), :]
    left_q = facts[pl.ds(first * MSG + 2, SPREAD, stride=MSG), :]
    lane = iota((1, TILE), 1)
    right_class = ((lane >> 2) + row) & (GROUP - 1)
    right_key = jnp.where(right_q > 0, (right_q - 1) * GROUP + right_class.astype(F32), -2.0)
    slot = iota((SPREAD, TILE), 1)
    left_class = (first + iota((SPREAD, TILE), 0) + ((slot * 43) >> 7)) & (GROUP - 1)
    left_key = jnp.where(left_q > 0, (left_q - 1) * GROUP + left_class.astype(F32), -1.0)
    partner = jnp.full((SPREAD, TILE), -1.0, F32)
    for t in range(GROUP * LEFT):
        partner = jnp.where(left_key[:, t : t + 1] == right_key, float(t), partner)
    kept = jnp.zeros((SPREAD, TILE), F32)
    for j in range(RIGHT):
        kept = kept + jnp.where(right_j == j + 1, keep[:, j : j + 1], 0.0)
    needed = jnp.where((partner >= 0) & (kept > 0), 1.0, 0.0)
    before = (iota((TILE, TILE), 0) < iota((TILE, TILE), 1)).astype(F32).astype(BF16)
    order = jnp.dot(needed.astype(BF16), before, preferred_element_type=F32)
    spread = (iota((TILE, 2 * TILE), 0) == (iota((TILE, 2 * TILE), 1) >> 1)).astype(F32).astype(BF16)
    needed2 = jnp.dot(needed.astype(BF16), spread, preferred_element_type=F32)
    order2 = jnp.dot(order.astype(BF16), spread, preferred_element_type=F32)
    half = (iota((SPREAD, 2 * TILE), 1) & 1).astype(F32)
    base_f = base.astype(F32)
    line = jnp.where(needed2 > 0, 2.0 * (order2 - base_f) + half, -1.0)
    lines = PIECE * PLACES
    chosen = line[:, None, :] == iota((SPREAD, lines, 2 * TILE), 1).astype(F32)
    chosen = jnp.where(chosen, 1.0, 0.0).reshape(SPREAD * lines, 2 * TILE).astype(BF16)
    held = pieces[:, :, 0 : WIDE * TILE].astype(F32).reshape(GROUP * MSG, WIDE * TILE).astype(BF16)
    packed = jnp.dot(chosen, held, preferred_element_type=F32)
    message[...] = packed.reshape(SPREAD, lines, WIDE * TILE).astype(BF16)
    most = jnp.max(jnp.where(needed > 0, order + 1.0, 0.0))
    own = iota((SPREAD, TILE), 0) == col - first
    own_order = jnp.sum(jnp.where(own & (needed > 0), order + 1.0, 0.0), axis=0, keepdims=True)
    own_partner = jnp.sum(jnp.where(own, partner, 0.0), axis=0, keepdims=True)
    at = iota((PLACES, TILE), 0).astype(F32) + 1.0 + base_f
    here = own_order == at
    left_slot = jnp.sum(jnp.where(here, own_partner, 0.0), axis=1, keepdims=True)
    block = jnp.sum(jnp.where(here, right_j - 1.0, 0.0), axis=1, keepdims=True)
    live = jnp.sum(jnp.where(here, 1.0, 0.0), axis=1, keepdims=True)
    lane = iota((PLACES, TILE), 1)
    wanted[...] = jnp.where(
        lane == 0, left_slot, jnp.where(lane == 1, block, jnp.where(lane == 2, live, most))
    ).astype(I32)


def product_kernel(place, wanted, left_here, left_there, pieces, start, out, rows, total):
    lines = PIECE * PLACES
    for v in range(WIDE):
        rows[v, 0 : SPREAD * lines, :] = pieces[:, :, v * TILE : (v + 1) * TILE].astype(F32).reshape(SPREAD * lines, TILE)
    if start is None:
        total[...] = jnp.zeros_like(total)
    else:
        total[...] = start[...]
    core = place[0] & 1
    for p in range(PLACES):

        @pl.when(wanted[p, 2] > 0)
        def _(p=p):
            tile = jnp.concatenate(
                [rows[u % WIDE, pl.ds(PIECE * p + u // WIDE, SPREAD, stride=lines), :] for u in range(TILE // SPREAD)],
                axis=0,
            ).astype(BF16)
            slot = wanted[p, 0]
            source = (slot * 43) >> 7
            a = pl.multiple_of((slot - source * LEFT) * TILE, TILE)
            panel = ((((place[0] >> 3) - (source >> 3)) & 3) << 2) + ((source >> 1) & 3)
            columns = pl.ds(pl.multiple_of(wanted[p, 1] * TILE, TILE), TILE)

            @pl.when((source & 1) == core)
            def _():
                total[:, columns] += jnp.dot(left_here[panel, pl.ds(a, TILE), :], tile, preferred_element_type=F32)

            @pl.when((source & 1) != core)
            def _():
                total[:, columns] += jnp.dot(left_there[panel, pl.ds(a, TILE), :], tile, preferred_element_type=F32)

    out[...] = total[...].astype(out.dtype)


def kernel_call(body, out_shape, scratch, spaces, *operands):
    kinds = {"s": pltpu.SMEM, "v": pltpu.VMEM, "a": pl.ANY}
    specs = [pl.BlockSpec(memory_space=kinds[space]) for space in spaces]
    many = isinstance(out_shape, tuple)
    vmem = pl.BlockSpec(memory_space=pltpu.VMEM)
    return pl.pallas_call(
        body,
        out_shape=out_shape,
        in_specs=specs,
        out_specs=tuple(vmem for _ in out_shape) if many else vmem,
        scratch_shapes=scratch,
        compiler_params=pltpu.CompilerParams(vmem_limit_bytes=VMEM_LIMIT),
    )(*operands)


def on_device(left_tiles, left_index, right_tiles, right_index, keep_mask):
    row, col = lax.axis_index(ROW), lax.axis_index(COL)
    place = jnp.stack([row, col, 0]).astype(I32)
    lines = PIECE * PLACES

    with jax.named_scope("left_ids"):
        key = left_index[0, 0, 1]
        values = jnp.where(key >= 0, lax.shift_right_logical(key, 5) + 1, 0)
        here = iota((LEFT, TILE), 1) == row * LEFT + iota((LEFT, TILE), 0)
        ids = jnp.sum(jnp.where(here, values[:, None], 0), axis=0).astype(F32).astype(BF16)
        near = ("y", "core")
        near_ids = jnp.broadcast_to(ids[None, None], (lax.axis_size(near), IDS, TILE))
        near_ids = lax.all_to_all(near_ids, near, 0, 0, tiled=True)

    with jax.named_scope("scatter_right"):
        data, own_facts = kernel_call(
            scatter_kernel,
            (
                jax.ShapeDtypeStruct((SPREAD, MSG, WIDE * TILE), BF16),
                jax.ShapeDtypeStruct((MSG, TILE), F32),
            ),
            [pltpu.VMEM((WIDE, (SPREAD + 1) * MSG, TILE), F32)],
            "sssv",
            place,
            right_index[0, 0],
            keep_mask,
            right_tiles[0, 0],
        )
    with jax.named_scope("left_zh"):
        payload = kernel_call(
            left_kernel,
            jax.ShapeDtypeStruct((PANEL + IDS, TILE), BF16),
            [],
            "vva",
            near_ids,
            left_tiles[0, 0],
            own_facts,
        )
        slab = lax.all_gather(payload, "zh")

    with jax.named_scope("right_message"):
        message = kernel_call(
            message_kernel,
            jax.ShapeDtypeStruct((GROUP, MSG, (WIDE + 1) * TILE), BF16),
            [],
            "vvv",
            data,
            own_facts,
            slab[:, PANEL:, :],
        )
        pieces = lax.all_to_all(message, COL, 0, 0, tiled=True)

    with jax.named_scope("left_y"):
        size = lax.axis_size("y")
        up = [(i, (i + 1) % size) for i in range(size)]
        down = [(i, (i - 1) % size) for i in range(size)]
        ring = [(2 * y + core, (y + 1 - 2 * core) % size * 2 + core) for y in range(size) for core in range(2)]
        below = lax.ppermute(slab, "y", up)
        above = lax.ppermute(slab, "y", down)
        onward = jnp.where(lax.axis_index("core") == 0, below, above)
        far = lax.ppermute(onward, ("y", "core"), ring)
        left_here = jnp.concatenate((slab, below, far, above))

    with jax.named_scope("left_core"):
        left_there = lax.ppermute(left_here, "core", [(0, 1), (1, 0)])

    def select(base):
        return kernel_call(
            select_kernel,
            (
                jax.ShapeDtypeStruct((SPREAD, lines, WIDE * TILE), BF16),
                jax.ShapeDtypeStruct((PLACES, TILE), I32),
            ),
            [pltpu.VMEM(((GROUP + 1) * MSG, TILE), F32)],
            "svaa",
            jnp.stack([row, col, base]).astype(I32),
            pieces,
            below,
            above,
        )

    def product(wanted, tiles, start, dtype):
        shape = (TILE, RIGHT * TILE)
        operands = (place, wanted, left_here, left_there, tiles) + (() if start is None else (start,))
        body = product_kernel
        if start is None:
            body = lambda a, b, c, d, e, out, *scratch: product_kernel(a, b, c, d, e, None, out, *scratch)
        return kernel_call(
            body,
            jax.ShapeDtypeStruct(shape, dtype),
            [pltpu.VMEM((WIDE, (SPREAD + 1) * lines, TILE), F32), pltpu.VMEM(shape, F32)],
            "ssvvvv"[: len(operands)],
            *operands,
        )

    with jax.named_scope("right_needed"):
        packed, wanted = select(jnp.int32(0))
        tiles = lax.all_to_all(packed, HALF, 0, 0, tiled=True)
    with jax.named_scope("multiply"):
        first = product(wanted, tiles, None, BF16)

    most = wanted[0, 3]

    def more_rounds(_):
        def one(carry):
            base, total = carry
            packed, wanted = select(base)
            tiles = lax.all_to_all(packed, HALF, 0, 0, tiled=True)
            return base + PLACES, product(wanted, tiles, total, F32)

        begin = (jnp.int32(0), jnp.zeros((TILE, RIGHT * TILE), F32))
        return lax.while_loop(lambda carry: carry[0] < most, one, begin)[1].astype(BF16)

    with jax.named_scope("further_rounds"):
        return lax.cond(most > PLACES, more_rounds, lambda done: done, first)


def solution(mesh):
    parts = Mesh(mesh.devices.reshape(4, 4, 2, 2, 4, 4), ROW + COL)
    in_specs = (P(COL, ROW), P(COL, ROW), P(ROW, COL), P(ROW, COL), P(COL, ROW))
    return jax.shard_map(on_device, mesh=parts, in_specs=in_specs, out_specs=P(COL, ROW), check_vma=False)
```
